32 devices in a mesh: ctx: 4 (over y, core), ch: 8 (over z, x).
Axes of the slice: x: 2, y: 2, z: 4, core: 2. Of those that a mesh axis runs over, the one named last changes fastest.
Arguments:
- tokens: bfloat16 [4096, 4096], P('ctx', 'ch'), may hold values from -6 to 6
- in_weight: bfloat16 [3, 4096, 4096], P(None, None, 'ch'), may hold values from -0.09375 to 0.09375
- short_filters: float32 [3, 3, 4096], P(None, None, 'ch'), may hold values from -3 to 3
- log_rates: float32 [16, 4096], P(None, 'ch'), may hold values from 0.1 to 500
- residues: float32 [16, 4096], P(None, 'ch'), may hold values from -0.06 to 0.06
- skip_gain: float32 [4096], P('ch'), may hold values from -4 to 4
- out_weight: bfloat16 [4096, 4096], P('ch'), may hold values from -0.125 to 0.125
Outputs:
- block_out: bfloat16 [4096, 4096], P('ctx', 'ch')
The draws below stay inside these ranges and needn't reach their ends.
All inputs are finite; a program needn't handle non-finite values.
Results may differ from the reference program's by a relative error of at most 0.008.
Values may be sent and summed in bfloat16 or wider, within the bound.
A program may use at most 192 MiB of HBM per device.

```python
import math
import jax
import jax.numpy as jnp
from jax import lax

D = 4096
MODES = 16
SHORT = 3
SEQ = 4096


def with_spikes(values, own_key, source, target, shards_of, factor):
    owner, partner = [(jnp.arange(values.shape[dim]) // (values.shape[dim] // shards_of)).reshape([-1 if axis == dim else 1 for axis in range(values.ndim)]) for dim in (source, target)]
    chosen = jax.random.permutation(own_key, shards_of)[partner]
    strong = (owner == chosen) | (owner == (partner + shards_of // 2) % shards_of)
    return jnp.where(strong, factor * values, values)


def levels(stream_key, shape, split, low, high):
    gain, own = 1.0, jax.random.fold_in(stream_key, 6)
    for position, parts in split:
        draws = jnp.exp(jax.random.uniform(jax.random.fold_in(own, position), (parts,), jnp.float32, low / len(split), high / len(split)))
        gain = gain * jnp.repeat(draws, shape[position] // parts).reshape([-1 if axis == position else 1 for axis in range(len(shape))])
    return gain


def scatter_about(rng, dims, deviation, most, cuts=(), kind=jnp.bfloat16):
    loudness = levels(rng, dims, cuts, -0.22, 0.18) if cuts else 1.0
    array = jax.random.normal(rng, dims, jnp.float32) * deviation * loudness
    return jnp.minimum(jnp.maximum(array, -most), most).astype(kind)


def noise_with(rng, shape, deviation, most, pieces, heavy, kind=jnp.bfloat16):
    drawn = deviation * jax.random.normal(rng, shape, jnp.float32)
    if pieces:
        drawn = drawn * levels(rng, shape, pieces, -0.22, 0.18)
    return jnp.clip(with_spikes(drawn, jax.random.fold_in(rng, 3), *heavy), -most, most).astype(kind)


def setup_inputs(seed: int = 0) -> dict:
    splits = jax.random.split(jax.random.key(seed), 8)
    return {
        "tokens": scatter_about(splits[0], (SEQ, D), 1.0, 6.0, ((0, 4), (1, 8))),
        "in_weight": scatter_about(splits[1], (3, D, D), D ** -0.5, 0.09375, ((2, 8),)),
        "short_filters": scatter_about(splits[2], (3, SHORT, D), 0.6, 3.0, ((2, 8),), jnp.float32),
        "log_rates": jnp.clip(jnp.exp(math.log(500.0) - 8.517193 * jax.random.uniform(splits[3], (MODES, D), jnp.float32) ** levels(splits[3], (MODES, D), ((1, 8),), -0.2, 0.2)), 0.1, 500.0),
        "residues": scatter_about(splits[4], (MODES, D), 0.01, 0.06, ((1, 8),), jnp.float32),
        "skip_gain": scatter_about(splits[5], (D,), 1.0, 4.0, ((0, 8),), jnp.float32),
        "out_weight": noise_with(splits[6], (D, D), D ** -0.5, 0.125, ((0, 8),), (0, 1, 8, 2.0)),
    }


def long_conv(mixed_in, log_rates, residues):
    seq = mixed_in.shape[0]
    width = mixed_in.shape[1]
    cols = min(256, width)
    count = width // cols
    zs = mixed_in.reshape(seq, count, cols).transpose(1, 0, 2)
    rates = log_rates.reshape(log_rates.shape[0], count, cols).transpose(1, 0, 2)
    weights = residues.reshape(residues.shape[0], count, cols).transpose(1, 0, 2)
    lags = jnp.arange(seq, dtype=jnp.float32)

    def one_block(items):
        zb, rb, wb = items
        kernel = jnp.sum(jnp.exp(-lags[:, None, None] * (rb / seq)[None]) * wb[None], axis=1)
        length = 2 * seq
        spectrum = jnp.fft.rfft(zb, length, axis=0) * jnp.fft.rfft(kernel, length, axis=0)
        return jnp.fft.irfft(spectrum, length, axis=0)[:seq].astype(zb.dtype)

    result = lax.map(one_block, (zs, rates, weights))
    return result.transpose(1, 0, 2).reshape(seq, width)


def reference(tokens, in_weight, short_filters, log_rates, residues, skip_gain, out_weight):
    projected = jnp.einsum('tk,pkc->ptc', tokens.astype(jnp.float32), in_weight.astype(jnp.float32)).astype(jnp.bfloat16)
    taps = short_filters.shape[1]
    seq = tokens.shape[0]
    extended = jnp.pad(projected.astype(jnp.float32), ((0, 0), (taps - 1, 0), (0, 0)))
    featured = jnp.zeros(projected.shape, jnp.float32)
    for lag in range(taps):
        featured = featured + short_filters[:, lag, None, :] * extended[:, taps - 1 - lag:taps - 1 - lag + seq, :]
    query, keyed, valued = featured[0], featured[1], featured[2]
    mixed_in = keyed * valued
    convolved = long_conv(mixed_in, log_rates, residues) + skip_gain[None, :] * mixed_in
    gated = (query * convolved).astype(jnp.bfloat16)
    return jnp.dot(gated, out_weight, preferred_element_type=jnp.float32).astype(jnp.bfloat16)
```

```python
import functools

import jax
import jax.numpy as jnp
from jax import lax
from jax.experimental import pallas as pl
from jax.experimental.pallas import tpu as pltpu
from jax.sharding import PartitionSpec as P

HALO = 16
TILE = 128


def features(part, start, size, proj_ref, filters_ref):
    window = proj_ref[part, pl.ds(start, size + HALO), :].astype(jnp.float32)
    total = None
    for lag in range(filters_ref.shape[1]):
        term = filters_ref[part, lag : lag + 1, :] * window[HALO - lag : HALO - lag + size]
        total = term if total is None else total + term
    return total


def state_kernel(seq, proj_ref, filters_ref, rates_ref, mixed_ref, state_ref):
    rows = mixed_ref.shape[0]
    decay = jnp.exp(rates_ref[...] * (-1.0 / seq))

    def tile(t, state):
        start = pl.multiple_of(t * TILE, TILE)
        keyed = features(1, start, TILE, proj_ref, filters_ref)
        valued = features(2, start, TILE, proj_ref, filters_ref)
        mixed_ref[pl.ds(start, TILE), :] = keyed * valued

        def group(g, state):
            base = pl.multiple_of(start + g * 8, 8)
            for i in range(8):
                state = decay * state + mixed_ref[pl.ds(base + i, 1), :]
            return state

        return lax.fori_loop(0, TILE // 8, group, state)

    state_ref[...] = lax.fori_loop(0, rows // TILE, tile, jnp.zeros_like(decay))


def conv_kernel(
    seq, proj_ref, mixed_ref, filters_ref, rates_ref, residues_ref, gain_ref, state_ref, out_ref, conv
):
    rows = mixed_ref.shape[0]
    decay = jnp.exp(rates_ref[...] * (-1.0 / seq))
    weight = residues_ref[...]
    gain = gain_ref[...]

    def tile(t, state):
        start = pl.multiple_of(t * TILE, TILE)

        def group(g, state):
            base = pl.multiple_of(start + g * 8, 8)
            parts = []
            for i in range(8):
                state = decay * state + mixed_ref[pl.ds(base + i, 1), :]
                parts.append(jnp.sum(weight * state, axis=0, keepdims=True))
            conv[pl.ds(pl.multiple_of(g * 8, 8), 8), :] = (
                jnp.concatenate(parts, 0) + gain * mixed_ref[pl.ds(base, 8), :]
            )
            return state

        state = lax.fori_loop(0, TILE // 8, group, state)
        query = features(0, start, TILE, proj_ref, filters_ref)
        out_ref[pl.ds(start, TILE), :] = (query * conv[...]).astype(out_ref.dtype)
        return state

    lax.fori_loop(0, rows // TILE, tile, state_ref[...])


def shards(tokens, in_weight, short_filters, log_rates, residues, skip_gain, out_weight):
    rows = tokens.shape[0]
    cols = in_weight.shape[2]
    ctx = lax.axis_size("ctx")
    seq = rows * ctx
    taps = short_filters.shape[1]
    modes = log_rates.shape[0]
    place = lax.axis_index("ctx")
    projected = jnp.einsum(
        "tk,pkc->ptc",
        lax.all_gather(tokens, "ch", axis=1, tiled=True),
        in_weight,
        preferred_element_type=jnp.float32,
    ).astype(jnp.bfloat16)
    previous = lax.ppermute(
        projected[:, rows - (taps - 1) :, :], "ctx", [(i, i + 1) for i in range(ctx - 1)]
    )
    extended = jnp.concatenate(
        [jnp.zeros((3, HALO - taps + 1, cols), jnp.bfloat16), previous, projected], axis=1
    )
    vmem = pl.BlockSpec(memory_space=pltpu.VMEM)
    params = pltpu.CompilerParams(vmem_limit_bytes=40 * 2**20)
    mixed, local = pl.pallas_call(
        functools.partial(state_kernel, seq),
        out_shape=(
            jax.ShapeDtypeStruct((rows, cols), jnp.float32),
            jax.ShapeDtypeStruct((modes, cols), jnp.float32),
        ),
        in_specs=[vmem] * 3,
        out_specs=(vmem, vmem),
        compiler_params=params,
    )(extended, short_filters, log_rates)
    gathered = lax.all_gather(local.astype(jnp.bfloat16), "ctx").astype(jnp.float32)
    hops = (place - 1 - jnp.arange(ctx))[:, None, None]
    spans = jnp.exp(-(log_rates / ctx)[None] * jnp.maximum(hops, 0).astype(jnp.float32))
    incoming = jnp.sum(jnp.where(hops >= 0, spans * gathered, 0.0), axis=0)
    gated = pl.pallas_call(
        functools.partial(conv_kernel, seq),
        out_shape=jax.ShapeDtypeStruct((rows, cols), jnp.bfloat16),
        in_specs=[vmem] * 7,
        out_specs=vmem,
        scratch_shapes=[pltpu.VMEM((TILE, cols), jnp.float32)],
        compiler_params=params,
    )(extended, mixed, short_filters, log_rates, residues, skip_gain[None, :], incoming)
    partial = jnp.dot(gated, out_weight, preferred_element_type=jnp.float32).astype(jnp.bfloat16)
    return lax.psum_scatter(partial, "ch", scatter_dimension=1, tiled=True)


def solution(mesh):
    return jax.shard_map(
        shards,
        mesh=mesh,
        in_specs=(
            P("ctx", "ch"),
            P(None, None, "ch"),
            P(None, None, "ch"),
            P(None, "ch"),
            P(None, "ch"),
            P("ch"),
            P("ch", None),
        ),
        out_specs=P("ctx", "ch"),
        check_vma=False,
    )
```

```python
import functools

import jax
import jax.numpy as jnp
from jax import lax
from jax.experimental import pallas as pl
from jax.experimental.pallas import tpu as pltpu
from jax.sharding import PartitionSpec as P

HALO = 16
TILE = 128
PIECE = 256


def features(part, start, size, proj_ref, filters_ref):
    window = proj_ref[part, pl.ds(start, size + HALO), :].astype(jnp.float32)
    total = None
    for lag in range(filters_ref.shape[1]):
        term = filters_ref[part, lag : lag + 1, :] * window[HALO - lag : HALO - lag + size]
        total = term if total is None else total + term
    return total


def remote(source, target, send, receive, device):
    return pltpu.make_async_remote_copy(
        src_ref=source,
        dst_ref=target,
        send_sem=send,
        recv_sem=receive,
        device_id=device,
        device_id_type=pl.DeviceIdType.MESH,
    )


def greet(outer, inner, place, count, ctx):
    barrier = pltpu.get_barrier_semaphore()

    def signal(device):
        pl.semaphore_signal(
            barrier, inc=1, device_id=device, device_id_type=pl.DeviceIdType.MESH
        )

    signal({"ch": outer * 2 + 1 - inner})

    @pl.when(outer > 0)
    def _():
        signal({"ch": (outer - 1) * 2 + inner})

    @pl.when(outer < count - 1)
    def _():
        signal({"ch": (outer + 1) * 2 + inner})

    for hop in range(1, ctx):
        signal({"ctx": lax.rem(place + hop, ctx)})
    near = (outer + count - 1) // count + (2 * count - 2 - outer) // count
    pl.semaphore_wait(barrier, ctx + near)


def project_kernel(
    count, ctx, tokens_ref, weight_ref, filters_ref, rates_ref,
    ext_ref, mixed_ref, incoming_ref,
    gath, weight, acc, halo, local, states,
    local_sem, send_z, send_x, recv, halo_sem, state_send, state_recv,
):
    place = lax.axis_index("ctx")
    me = lax.axis_index("ch")
    outer, inner = me // 2, lax.rem(me, 2)
    rows, depth = tokens_ref.shape
    seq = rows * ctx
    pieces = rows // PIECE
    own = pltpu.make_async_copy(tokens_ref, gath.at[me], local_sem.at[0])
    own.start()
    loads = [
        pltpu.make_async_copy(weight_ref.at[p], weight.at[p], local_sem.at[1 + p]) for p in range(3)
    ]
    for load in loads:
        load.start()
    greet(outer, inner, place, count, ctx)
    own.wait()

    def span(r):
        return pl.ds(pl.multiple_of(r * PIECE, PIECE), PIECE)

    def along(source, r, up):
        slot = source * 2 + inner
        block = gath.at[slot, span(r)]
        step = 1 if up else -1
        return remote(
            block, block, send_z.at[0 if up else 1, source, r], recv.at[slot, r],
            {"ch": (outer + step) * 2 + inner},
        )

    def across(source, r):
        slot = source * 2 + inner
        block = gath.at[slot, span(r)]
        return remote(
            block, block, send_x.at[source, r], recv.at[slot, r],
            {"ch": outer * 2 + 1 - inner},
        )

    def arrived(slot, r):
        block = gath.at[slot, span(r)]
        remote(block, block, send_x.at[0, 0], recv.at[slot, r], {"ch": outer * 2 + 1 - inner}).wait_recv()

    def multiply(slot, r, first=False):
        block = gath[slot, span(r), :]
        for p in range(3):
            term = jnp.dot(
                block,
                weight[p, pl.ds(pl.multiple_of(slot * depth, depth), depth), :],
                preferred_element_type=jnp.float32,
            )
            if first:
                acc[p, span(r), :] = term
            else:
                acc[p, span(r), :] += term

    def begin(r, carry):
        across(outer, r).start()

        @pl.when(outer < count - 1)
        def _():
            along(outer, r, True).start()

        @pl.when(outer > 0)
        def _():
            along(outer, r, False).start()

        return carry

    lax.fori_loop(0, pieces, begin, 0)
    for load in loads:
        load.wait()

    def start(r, carry):
        multiply(me, r, True)
        return carry

    lax.fori_loop(0, pieces, start, 0)

    def take(slot, r):
        arrived(slot, r)
        multiply(slot, r)

    def beside(distance):
        other = 1 - inner

        def one(r, carry):
            if distance == 0:
                take(outer * 2 + other, r)
                return carry

            @pl.when(outer >= distance)
            def _():
                take((outer - distance) * 2 + other, r)

            @pl.when(outer + distance < count)
            def _():
                take((outer + distance) * 2 + other, r)

            return carry

        lax.fori_loop(0, pieces, one, 0)

    for distance in range(1, count):

        def one(r, carry, distance=distance):
            @pl.when(outer >= distance)
            def _():
                source = outer - distance
                arrived(source * 2 + inner, r)

                @pl.when(outer < count - 1)
                def _():
                    along(source, r, True).start()

                across(source, r).start()
                multiply(source * 2 + inner, r)

            @pl.when(outer + distance < count)
            def _():
                source = outer + distance
                arrived(source * 2 + inner, r)

                @pl.when(outer > 0)
                def _():
                    along(source, r, False).start()

                across(source, r).start()
                multiply(source * 2 + inner, r)

            return carry

        lax.fori_loop(0, pieces, one, 0)
        beside(distance - 1)
    beside(count - 1)

    def settle(t, carry):
        base = pl.multiple_of(rows - (t + 1) * TILE, TILE)
        for p in range(3):
            ext_ref[p, pl.ds(HALO + base, TILE), :] = acc[p, pl.ds(base, TILE), :].astype(ext_ref.dtype)
        return carry

    settle(0, 0)
    edge = remote(
        ext_ref.at[:, pl.ds(rows, HALO), :], halo, halo_sem.at[0], halo_sem.at[1],
        {"ctx": lax.rem(place + 1, ctx)},
    )

    @pl.when(place < ctx - 1)
    def _():
        edge.start()

    lax.fori_loop(1, rows // TILE, settle, 0)

    @pl.when(place > 0)
    def _():
        edge.wait_recv()
        ext_ref[:, :HALO, :] = halo[...]

    @pl.when(place == 0)
    def _():
        ext_ref[:, :HALO, :] = jnp.zeros_like(halo)

    rate = rates_ref[...]
    decay = jnp.exp(rate * (-1.0 / seq))

    def tile(t, state):
        base = pl.multiple_of(t * TILE, TILE)
        keyed = features(1, base, TILE, ext_ref, filters_ref)
        valued = features(2, base, TILE, ext_ref, filters_ref)
        mixed_ref[pl.ds(base, TILE), :] = keyed * valued

        def group(g, state):
            row = pl.multiple_of(base + g * 8, 8)
            for i in range(8):
                state = decay * state + mixed_ref[pl.ds(row + i, 1), :]
            return state

        return lax.fori_loop(0, TILE // 8, group, state)

    local[...] = lax.fori_loop(0, rows // TILE, tile, jnp.zeros_like(decay))
    sends = [
        remote(
            local, states.at[hop - 1], state_send.at[hop - 1], state_recv.at[hop - 1],
            {"ctx": lax.rem(place + hop, ctx)},
        )
        for hop in range(1, ctx)
    ]
    for send in sends:
        send.start()
    total = jnp.zeros_like(decay)
    for hop in range(1, ctx):
        sends[hop - 1].wait_recv()
        term = jnp.exp(rate * (-(hop - 1) / ctx)) * states[hop - 1]
        total = total + jnp.where(place >= hop, term, 0.0)
    incoming_ref[...] = total
    for send in sends:
        send.wait_send()

    @pl.when(place < ctx - 1)
    def _():
        edge.wait_send()

    def drain(r, carry):
        for source in range(count):
            across(source, r).wait_send()

            @pl.when(jnp.logical_and(outer >= source, outer < count - 1))
            def _():
                along(source, r, True).wait_send()

            @pl.when(jnp.logical_and(outer <= source, outer > 0))
            def _():
                along(source, r, False).wait_send()

        return carry

    lax.fori_loop(0, pieces, drain, 0)


def output_kernel(
    count, ctx, ext_ref, mixed_ref, filters_ref, rates_ref, residues_ref, gain_ref, state_ref,
    weight_ref, out_ref,
    conv, gated, stage, beside, chain, send_x, recv_x, send_z, recv_z,
):
    me = lax.axis_index("ch")
    outer, inner = me // 2, lax.rem(me, 2)
    rows, width = out_ref.shape
    seq = rows * ctx
    pieces = rows // PIECE
    greet(outer, inner, 0, count, 1)
    decay = jnp.exp(rates_ref[...] * (-1.0 / seq))
    residue = residues_ref[...]
    gain = gain_ref[...]
    far = (count - 1) * (1 - outer // (count // 2))

    def span(r):
        return pl.ds(pl.multiple_of(r * PIECE, PIECE), PIECE)

    def partial(block, r):
        return jnp.dot(
            gated[span(r), :],
            weight_ref[:, pl.ds(pl.multiple_of(block * width, width), width)],
            preferred_element_type=jnp.float32,
        )

    def across(target, r):
        return remote(
            stage.at[target, span(r)], beside.at[target, span(r)],
            send_x.at[target, r], recv_x.at[target, r],
            {"ch": outer * 2 + 1 - inner},
        )

    def along(target, r, up, last):
        slot = count if last and not up else target
        step = 1 if up else -1
        return remote(
            beside.at[target, span(r)], chain.at[slot, span(r)],
            send_z.at[target, r], recv_z.at[slot, r],
            {"ch": (outer + step) * 2 + inner},
        )

    def received(slot, r):
        block = chain.at[slot, span(r)]
        remote(
            block, block, send_z.at[0, 0], recv_z.at[slot, r], {"ch": outer * 2 + 1 - inner}
        ).wait_recv()
        return chain[slot, span(r), :].astype(jnp.float32)

    def give(target, r):
        stage[target, span(r), :] = partial(target * 2 + 1 - inner, r).astype(stage.dtype)
        across(target, r).start()

    def first(r, state):
        base = pl.multiple_of(r * PIECE, PIECE)

        def group(g, state):
            row = pl.multiple_of(base + g * 8, 8)
            parts = []
            for i in range(8):
                state = decay * state + mixed_ref[pl.ds(row + i, 1), :]
                parts.append(jnp.sum(residue * state, axis=0, keepdims=True))
            conv[pl.ds(pl.multiple_of(g * 8, 8), 8), :] = (
                jnp.concatenate(parts, 0) + gain * mixed_ref[pl.ds(row, 8), :]
            )
            return state

        state = lax.fori_loop(0, PIECE // 8, group, state)
        query = features(0, base, PIECE, ext_ref, filters_ref)
        gated[span(r), :] = (query * conv[...]).astype(gated.dtype)
        give(far, r)
        return state

    lax.fori_loop(0, pieces, first, state_ref[...])
    for distance in range(count - 2, -1, -1):

        def rest(r, carry, distance=distance):
            @pl.when(jnp.logical_and(outer + distance < count, outer + distance != far))
            def _():
                give(outer + distance, r)

            if distance:

                @pl.when(jnp.logical_and(outer >= distance, outer - distance != far))
                def _():
                    give(outer - distance, r)

            return carry

        lax.fori_loop(0, pieces, rest, 0)

    def total(target, r):
        mine = partial(target * 2 + inner, r)
        across(target, r).wait_recv()
        return mine + beside[target, span(r), :].astype(jnp.float32)

    for distance in range(count - 1, 0, -1):

        def hop(r, carry, distance=distance):
            @pl.when(outer + distance < count)
            def _():
                target = outer + distance
                conv[...] = total(target, r)

                @pl.when(outer > 0)
                def _():
                    conv[...] += received(target, r)

                beside[target, span(r), :] = conv[...].astype(beside.dtype)
                along(target, r, True, distance == 1).start()

            @pl.when(outer >= distance)
            def _():
                target = outer - distance
                conv[...] = total(target, r)

                @pl.when(outer < count - 1)
                def _():
                    conv[...] += received(target, r)

                beside[target, span(r), :] = conv[...].astype(beside.dtype)
                along(target, r, False, distance == 1).start()

            return carry

        lax.fori_loop(0, pieces, hop, 0)

    def finish(r, carry):
        conv[...] = total(outer, r)

        @pl.when(outer > 0)
        def _():
            conv[...] += received(outer, r)

        @pl.when(outer < count - 1)
        def _():
            conv[...] += received(count, r)

        out_ref[span(r), :] = conv[...].astype(out_ref.dtype)
        return carry

    lax.fori_loop(0, pieces, finish, 0)

    def drain(r, carry):
        for target in range(count):
            across(target, r).wait_send()

            @pl.when(outer != target)
            def _():
                along(target, r, True, False).wait_send()

        return carry

    lax.fori_loop(0, pieces, drain, 0)


def shards(tokens, in_weight, short_filters, log_rates, residues, skip_gain, out_weight):
    rows, depth = tokens.shape
    cols = in_weight.shape[2]
    ctx = lax.axis_size("ctx")
    ways = lax.axis_size("ch")
    count = ways // 2
    modes = log_rates.shape[0]
    pieces = rows // PIECE
    vmem = pl.BlockSpec(memory_space=pltpu.VMEM)
    anywhere = pl.BlockSpec(memory_space=pl.ANY)
    dma = pltpu.SemaphoreType.DMA
    f32, bf16 = jnp.float32, jnp.bfloat16
    extended, mixed, incoming = pl.pallas_call(
        functools.partial(project_kernel, count, ctx),
        out_shape=(
            jax.ShapeDtypeStruct((3, HALO + rows, cols), bf16),
            jax.ShapeDtypeStruct((rows, cols), f32),
            jax.ShapeDtypeStruct((modes, cols), f32),
        ),
        in_specs=[anywhere, anywhere, vmem, vmem],
        out_specs=(vmem, vmem, vmem),
        scratch_shapes=[
            pltpu.VMEM((ways, rows, depth), bf16),
            pltpu.VMEM((3, ways * depth, cols), bf16),
            pltpu.VMEM((3, rows, cols), f32),
            pltpu.VMEM((3, HALO, cols), bf16),
            pltpu.VMEM((modes, cols), f32),
            pltpu.VMEM((ctx - 1, modes, cols), f32),
            dma((4,)),
            dma((2, count, pieces)),
            dma((count, pieces)),
            dma((ways, pieces)),
            dma((2,)),
            dma((ctx - 1,)),
            dma((ctx - 1,)),
        ],
        compiler_params=pltpu.CompilerParams(
            collective_id=0, has_side_effects=True, vmem_limit_bytes=48 * 2**20
        ),
    )(tokens, in_weight, short_filters, log_rates)
    return pl.pallas_call(
        functools.partial(output_kernel, count, ctx),
        out_shape=jax.ShapeDtypeStruct((rows, depth), bf16),
        in_specs=[vmem] * 8,
        out_specs=vmem,
        scratch_shapes=[
            pltpu.VMEM((PIECE, cols), f32),
            pltpu.VMEM((rows, cols), bf16),
            pltpu.VMEM((count, rows, depth), bf16),
            pltpu.VMEM((count, rows, depth), bf16),
            pltpu.VMEM((count + 1, rows, depth), bf16),
            dma((count, pieces)),
            dma((count, pieces)),
            dma((count, pieces)),
            dma((count + 1, pieces)),
        ],
        compiler_params=pltpu.CompilerParams(
            collective_id=1, has_side_effects=True, vmem_limit_bytes=48 * 2**20
        ),
    )(
        extended, mixed, short_filters, log_rates, residues, skip_gain[None, :], incoming, out_weight
    )


def solution(mesh):
    return jax.shard_map(
        shards,
        mesh=mesh,
        in_specs=(
            P("ctx", "ch"),
            P(None, None, "ch"),
            P(None, None, "ch"),
            P(None, "ch"),
            P(None, "ch"),
            P("ch"),
            P("ch", None),
        ),
        out_specs=P("ctx", "ch"),
        check_vma=False,
    )
```

```python
import functools

import jax
import jax.numpy as jnp
from jax import lax
from jax.experimental import pallas as pl
from jax.experimental.pallas import tpu as pltpu
from jax.sharding import PartitionSpec as P

HALO = 16
TILE = 128
PIECE = 256


def features(part, start, size, proj_ref, filters_ref):
    window = proj_ref[part, pl.ds(start, size + HALO), :].astype(jnp.float32)
    total = None
    for lag in range(filters_ref.shape[1]):
        term = filters_ref[part, lag : lag + 1, :] * window[HALO - lag : HALO - lag + size]
        total = term if total is None else total + term
    return total


def remote(source, target, send, receive, device):
    return pltpu.make_async_remote_copy(
        src_ref=source,
        dst_ref=target,
        send_sem=send,
        recv_sem=receive,
        device_id=device,
        device_id_type=pl.DeviceIdType.MESH,
    )


def greet(outer, inner, place, count, ctx):
    barrier = pltpu.get_barrier_semaphore()

    def signal(device):
        pl.semaphore_signal(
            barrier, inc=1, device_id=device, device_id_type=pl.DeviceIdType.MESH
        )

    signal({"ch": outer * 2 + 1 - inner})

    @pl.when(outer > 0)
    def _():
        signal({"ch": (outer - 1) * 2 + inner})

    @pl.when(outer < count - 1)
    def _():
        signal({"ch": (outer + 1) * 2 + inner})

    for hop in range(1, ctx):
        signal({"ctx": lax.rem(place + hop, ctx)})
    near = (outer + count - 1) // count + (2 * count - 2 - outer) // count
    pl.semaphore_wait(barrier, ctx + near)


def project_kernel(
    count, ctx, tokens_ref, weight_ref, filters_ref, rates_ref,
    ext_ref, mixed_ref, incoming_ref,
    gath, weight, acc, halo, local, states,
    local_sem, send_z, send_x, recv, halo_sem, state_send, state_recv, send_pair,
):
    place = lax.axis_index("ctx")
    me = lax.axis_index("ch")
    outer, inner = me // 2, lax.rem(me, 2)
    rows, depth = tokens_ref.shape
    seq = rows * ctx
    pieces = rows // PIECE
    half = pieces // 2
    pair = outer + 1 - 2 * lax.rem(outer, 2)
    own = pltpu.make_async_copy(tokens_ref, gath.at[me], local_sem.at[0])
    own.start()
    loads = [
        pltpu.make_async_copy(weight_ref.at[p], weight.at[p], local_sem.at[1 + p]) for p in range(3)
    ]
    for load in loads:
        load.start()
    greet(outer, inner, place, count, ctx)
    own.wait()

    def span(r):
        return pl.ds(pl.multiple_of(r * PIECE, PIECE), PIECE)

    def along(source, r, up):
        slot = source * 2 + inner
        block = gath.at[slot, span(r)]
        step = 1 if up else -1
        return remote(
            block, block, send_z.at[0 if up else 1, source, r], recv.at[slot, r],
            {"ch": (outer + step) * 2 + inner},
        )

    def across(source, r):
        slot = source * 2 + inner
        block = gath.at[slot, span(r)]
        return remote(
            block, block, send_x.at[source, r], recv.at[slot, r],
            {"ch": outer * 2 + 1 - inner},
        )

    def cross(source, r):
        @pl.when(jnp.logical_or(source != pair, r >= half))
        def _():
            across(source, r).start()

    def relay(r):
        block = gath.at[outer * 2 + 1 - inner, span(r)]
        return remote(
            block, block, send_pair.at[r], recv.at[outer * 2 + 1 - inner, r],
            {"ch": pair * 2 + inner},
        )

    def arrived(slot, r):
        block = gath.at[slot, span(r)]
        remote(block, block, send_x.at[0, 0], recv.at[slot, r], {"ch": outer * 2 + 1 - inner}).wait_recv()

    def multiply(slot, r, first=False):
        block = gath[slot, span(r), :]
        for p in range(3):
            term = jnp.dot(
                block,
                weight[p, pl.ds(pl.multiple_of(slot * depth, depth), depth), :],
                preferred_element_type=jnp.float32,
            )
            if first:
                acc[p, span(r), :] = term
            else:
                acc[p, span(r), :] += term

    def begin(r, carry):
        across(outer, r).start()

        @pl.when(outer < count - 1)
        def _():
            along(outer, r, True).start()

        @pl.when(outer > 0)
        def _():
            along(outer, r, False).start()

        return carry

    lax.fori_loop(0, pieces, begin, 0)
    for load in loads:
        load.wait()

    def start(r, carry):
        multiply(me, r, True)
        return carry

    lax.fori_loop(0, pieces, start, 0)

    def take(slot, r):
        arrived(slot, r)
        multiply(slot, r)

    def direct(source, r):
        return jnp.logical_or(source != pair, r >= half)

    def beside(distance):
        other = 1 - inner

        def one(r, carry):
            if distance == 0:
                take(outer * 2 + other, r)
                return carry

            @pl.when(jnp.logical_and(outer >= distance, direct(outer - distance, r)))
            def _():
                take((outer - distance) * 2 + other, r)

            @pl.when(jnp.logical_and(outer + distance < count, direct(outer + distance, r)))
            def _():
                take((outer + distance) * 2 + other, r)

            return carry

        lax.fori_loop(0, pieces, one, 0)

    for distance in range(1, count):

        def one(r, carry, distance=distance):
            @pl.when(outer >= distance)
            def _():
                source = outer - distance
                arrived(source * 2 + inner, r)

                @pl.when(outer < count - 1)
                def _():
                    along(source, r, True).start()

                cross(source, r)
                multiply(source * 2 + inner, r)

            @pl.when(outer + distance < count)
            def _():
                source = outer + distance
                arrived(source * 2 + inner, r)

                @pl.when(outer > 0)
                def _():
                    along(source, r, False).start()

                cross(source, r)
                multiply(source * 2 + inner, r)

            return carry

        lax.fori_loop(0, pieces, one, 0)
        if distance == count - 1:
            for r in range(half):
                relay(r).start()
        beside(distance - 1)
    beside(count - 1)

    def last(r, carry):
        take(pair * 2 + 1 - inner, r)
        return carry

    lax.fori_loop(0, half, last, 0)

    def settle(t, carry):
        base = pl.multiple_of(rows - (t + 1) * TILE, TILE)
        for p in range(3):
            ext_ref[p, pl.ds(HALO + base, TILE), :] = acc[p, pl.ds(base, TILE), :].astype(ext_ref.dtype)
        return carry

    settle(0, 0)
    edge = remote(
        ext_ref.at[:, pl.ds(rows, HALO), :], halo, halo_sem.at[0], halo_sem.at[1],
        {"ctx": lax.rem(place + 1, ctx)},
    )

    @pl.when(place < ctx - 1)
    def _():
        edge.start()

    lax.fori_loop(1, rows // TILE, settle, 0)

    @pl.when(place > 0)
    def _():
        edge.wait_recv()
        ext_ref[:, :HALO, :] = halo[...]

    @pl.when(place == 0)
    def _():
        ext_ref[:, :HALO, :] = jnp.zeros_like(halo)

    rate = rates_ref[...]
    decay = jnp.exp(rate * (-1.0 / seq))

    def tile(t, state):
        base = pl.multiple_of(t * TILE, TILE)
        keyed = features(1, base, TILE, ext_ref, filters_ref)
        valued = features(2, base, TILE, ext_ref, filters_ref)
        mixed_ref[pl.ds(base, TILE), :] = keyed * valued

        def group(g, state):
            row = pl.multiple_of(base + g * 8, 8)
            for i in range(8):
                state = decay * state + mixed_ref[pl.ds(row + i, 1), :]
            return state

        return lax.fori_loop(0, TILE // 8, group, state)

    local[...] = lax.fori_loop(0, rows // TILE, tile, jnp.zeros_like(decay))
    sends = [
        remote(
            local, states.at[hop - 1], state_send.at[hop - 1], state_recv.at[hop - 1],
            {"ctx": lax.rem(place + hop, ctx)},
        )
        for hop in range(1, ctx)
    ]
    for send in sends:
        send.start()
    total = jnp.zeros_like(decay)
    for hop in range(1, ctx):
        sends[hop - 1].wait_recv()
        term = jnp.exp(rate * (-(hop - 1) / ctx)) * states[hop - 1]
        total = total + jnp.where(place >= hop, term, 0.0)
    incoming_ref[...] = total
    for send in sends:
        send.wait_send()

    @pl.when(place < ctx - 1)
    def _():
        edge.wait_send()

    def drain(r, carry):
        for source in range(count):

            @pl.when(direct(source, r))
            def _():
                across(source, r).wait_send()

            @pl.when(jnp.logical_and(outer >= source, outer < count - 1))
            def _():
                along(source, r, True).wait_send()

            @pl.when(jnp.logical_and(outer <= source, outer > 0))
            def _():
                along(source, r, False).wait_send()

        return carry

    lax.fori_loop(0, pieces, drain, 0)
    for r in range(half):
        relay(r).wait_send()


def output_kernel(
    count, ctx, ext_ref, mixed_ref, filters_ref, rates_ref, residues_ref, gain_ref, state_ref,
    weight_ref, out_ref,
    conv, gated, stage, beside, chain, send_x, recv_x, send_z, recv_z, passed, recv_pair,
):
    me = lax.axis_index("ch")
    outer, inner = me // 2, lax.rem(me, 2)
    rows, width = out_ref.shape
    seq = rows * ctx
    pieces = rows // PIECE
    half = pieces // 2
    pair = outer + 1 - 2 * lax.rem(outer, 2)
    greet(outer, inner, 0, count, 1)
    decay = jnp.exp(rates_ref[...] * (-1.0 / seq))
    residue = residues_ref[...]
    gain = gain_ref[...]
    far = (count - 1) * (1 - outer // (count // 2))

    def span(r):
        return pl.ds(pl.multiple_of(r * PIECE, PIECE), PIECE)

    def partial(block, r):
        return jnp.dot(
            gated[span(r), :],
            weight_ref[:, pl.ds(pl.multiple_of(block * width, width), width)],
            preferred_element_type=jnp.float32,
        )

    def across(target, r):
        return remote(
            stage.at[target, span(r)], beside.at[target, span(r)],
            send_x.at[target, r], recv_x.at[target, r],
            {"ch": outer * 2 + 1 - inner},
        )

    def along(target, r, up, last):
        slot = count if last and not up else target
        step = 1 if up else -1
        return remote(
            beside.at[target, span(r)], chain.at[slot, span(r)],
            send_z.at[target, r], recv_z.at[slot, r],
            {"ch": (outer + step) * 2 + inner},
        )

    def relay(r):
        return remote(
            stage.at[pair, span(r)], passed.at[span(r)], send_x.at[pair, r], recv_pair.at[r],
            {"ch": pair * 2 + inner},
        )

    def received(slot, r):
        block = chain.at[slot, span(r)]
        remote(
            block, block, send_z.at[0, 0], recv_z.at[slot, r], {"ch": outer * 2 + 1 - inner}
        ).wait_recv()
        return chain[slot, span(r), :].astype(jnp.float32)

    def give(target, r):
        stage[target, span(r), :] = partial(target * 2 + 1 - inner, r).astype(stage.dtype)

        @pl.when(jnp.logical_or(target != pair, r >= half))
        def _():
            across(target, r).start()

        @pl.when(jnp.logical_and(target == pair, r < half))
        def _():
            relay(r).start()

    def give_joined(r, carry):
        relay(r).wait_recv()
        stage[outer, span(r), :] = (
            partial(outer * 2 + 1 - inner, r) + passed[span(r), :].astype(jnp.float32)
        ).astype(stage.dtype)
        across(outer, r).start()
        return carry

    def first(r, state):
        base = pl.multiple_of(r * PIECE, PIECE)

        def group(g, state):
            row = pl.multiple_of(base + g * 8, 8)
            parts = []
            for i in range(8):
                state = decay * state + mixed_ref[pl.ds(row + i, 1), :]
                parts.append(jnp.sum(residue * state, axis=0, keepdims=True))
            conv[pl.ds(pl.multiple_of(g * 8, 8), 8), :] = (
                jnp.concatenate(parts, 0) + gain * mixed_ref[pl.ds(row, 8), :]
            )
            return state

        state = lax.fori_loop(0, PIECE // 8, group, state)
        query = features(0, base, PIECE, ext_ref, filters_ref)
        gated[span(r), :] = (query * conv[...]).astype(gated.dtype)
        give(far, r)
        return state

    lax.fori_loop(0, pieces, first, state_ref[...])
    for distance in range(count - 2, -1, -1):

        def rest(r, carry, distance=distance):
            if distance == 0:

                @pl.when(r >= half)
                def _():
                    give(outer, r)

            if distance:

                @pl.when(jnp.logical_and(outer + distance < count, outer + distance != far))
                def _():
                    give(outer + distance, r)

                @pl.when(jnp.logical_and(outer >= distance, outer - distance != far))
                def _():
                    give(outer - distance, r)

            return carry

        lax.fori_loop(0, pieces, rest, 0)

    def total(target, r):
        conv[...] = partial(target * 2 + inner, r)

        @pl.when(jnp.logical_or(target != pair, r >= half))
        def _():
            across(target, r).wait_recv()
            conv[...] += beside[target, span(r), :].astype(jnp.float32)

    for distance in range(count - 1, 0, -1):

        def hop(r, carry, distance=distance):
            @pl.when(outer + distance < count)
            def _():
                target = outer + distance
                total(target, r)

                @pl.when(outer > 0)
                def _():
                    conv[...] += received(target, r)

                beside[target, span(r), :] = conv[...].astype(beside.dtype)
                along(target, r, True, distance == 1).start()

            @pl.when(outer >= distance)
            def _():
                target = outer - distance
                total(target, r)

                @pl.when(outer < count - 1)
                def _():
                    conv[...] += received(target, r)

                beside[target, span(r), :] = conv[...].astype(beside.dtype)
                along(target, r, False, distance == 1).start()

            return carry

        lax.fori_loop(0, pieces, hop, 0)
        if distance == max(count - 2, 1):
            lax.fori_loop(0, half, give_joined, 0)

    def finish(r, carry):
        total(outer, r)

        @pl.when(outer > 0)
        def _():
            conv[...] += received(outer, r)

        @pl.when(outer < count - 1)
        def _():
            conv[...] += received(count, r)

        out_ref[span(r), :] = conv[...].astype(out_ref.dtype)
        return carry

    lax.fori_loop(0, pieces, finish, 0)

    def drain(r, carry):
        for target in range(count):
            across(target, r).wait_send()

            @pl.when(outer != target)
            def _():
                along(target, r, True, False).wait_send()

        return carry

    lax.fori_loop(0, pieces, drain, 0)


def shards(tokens, in_weight, short_filters, log_rates, residues, skip_gain, out_weight):
    rows, depth = tokens.shape
    cols = in_weight.shape[2]
    ctx = lax.axis_size("ctx")
    ways = lax.axis_size("ch")
    count = ways // 2
    modes = log_rates.shape[0]
    pieces = rows // PIECE
    vmem = pl.BlockSpec(memory_space=pltpu.VMEM)
    anywhere = pl.BlockSpec(memory_space=pl.ANY)
    dma = pltpu.SemaphoreType.DMA
    f32, bf16 = jnp.float32, jnp.bfloat16
    extended, mixed, incoming = pl.pallas_call(
        functools.partial(project_kernel, count, ctx),
        out_shape=(
            jax.ShapeDtypeStruct((3, HALO + rows, cols), bf16),
            jax.ShapeDtypeStruct((rows, cols), f32),
            jax.ShapeDtypeStruct((modes, cols), f32),
        ),
        in_specs=[anywhere, anywhere, vmem, vmem],
        out_specs=(vmem, vmem, vmem),
        scratch_shapes=[
            pltpu.VMEM((ways, rows, depth), bf16),
            pltpu.VMEM((3, ways * depth, cols), bf16),
            pltpu.VMEM((3, rows, cols), f32),
            pltpu.VMEM((3, HALO, cols), bf16),
            pltpu.VMEM((modes, cols), f32),
            pltpu.VMEM((ctx - 1, modes, cols), f32),
            dma((4,)),
            dma((2, count, pieces)),
            dma((count, pieces)),
            dma((ways, pieces)),
            dma((2,)),
            dma((ctx - 1,)),
            dma((ctx - 1,)),
            dma((max(1, pieces // 2),)),
        ],
        compiler_params=pltpu.CompilerParams(
            collective_id=0, has_side_effects=True, vmem_limit_bytes=48 * 2**20
        ),
    )(tokens, in_weight, short_filters, log_rates)
    return pl.pallas_call(
        functools.partial(output_kernel, count, ctx),
        out_shape=jax.ShapeDtypeStruct((rows, depth), bf16),
        in_specs=[vmem] * 8,
        out_specs=vmem,
        scratch_shapes=[
            pltpu.VMEM((PIECE, cols), f32),
            pltpu.VMEM((rows, cols), bf16),
            pltpu.VMEM((count, rows, depth), bf16),
            pltpu.VMEM((count, rows, depth), bf16),
            pltpu.VMEM((count + 1, rows, depth), bf16),
            dma((count, pieces)),
            dma((count, pieces)),
            dma((count, pieces)),
            dma((count + 1, pieces)),
            pltpu.VMEM((rows, depth), bf16),
            dma((pieces,)),
        ],
        compiler_params=pltpu.CompilerParams(
            collective_id=1, has_side_effects=True, vmem_limit_bytes=48 * 2**20
        ),
    )(
        extended, mixed, short_filters, log_rates, residues, skip_gain[None, :], incoming, out_weight
    )


def solution(mesh):
    return jax.shard_map(
        shards,
        mesh=mesh,
        in_specs=(
            P("ctx", "ch"),
            P(None, None, "ch"),
            P(None, None, "ch"),
            P(None, "ch"),
            P(None, "ch"),
            P("ch"),
            P("ch", None),
        ),
        out_specs=P("ctx", "ch"),
        check_vma=False,
    )
```
